32 devices in a mesh: group: 2 (over x), expert: 4 (over z), hid: 4 (over y, core).
Axes of the slice: x: 2, y: 2, z: 4, core: 2. Of those that a mesh axis runs over, the one named last changes fastest.
Arguments:
- tokens: bfloat16 [256, 4096], P(('group', 'expert', 'hid')), may hold values from -6 to 6
- expert_ids: int32 [256, 2], P(('group', 'expert', 'hid')), may hold values from 0 to 7, all different within a row; in each aligned block of 8 rows (0 to 7, 8 to 15, ...) at most 4 rows name the same one
- gate_numer: int32 [256, 2], P(('group', 'expert', 'hid')), may hold values from 8 to 64
- gate_weight: bfloat16 [8, 4096, 14336], P('group', None, ('expert', 'hid')), may hold values from -0.09375 to 0.09375
- up_weight: bfloat16 [8, 4096, 14336], P('group', None, ('expert', 'hid')), may hold values from -0.09375 to 0.09375
- down_weight: bfloat16 [8, 14336, 4096], P('group', ('expert', 'hid')), may hold values from -0.046875 to 0.046875
Outputs:
- mixed: bfloat16 [256, 4096], P(('group', 'expert', 'hid'))
The draws below stay inside these ranges and needn't reach their ends.
Inputs may be any that keep to these rules, and one draw needn't show every extreme that they name: `expert_ids`: A token's 2 ids differ. Within the rows of one device (aligned blocks of 8 rows) no expert is named more than 4 times, and in every draw some block names some expert exactly 4 times.
All inputs are finite; a program needn't handle non-finite values.
Results may differ from the reference program's by a relative error of at most 0.018.
Values may be sent and summed in bfloat16 or wider, within the bound.
A program may use at most 192 MiB of HBM per device.

```python
import math
import jax
import jax.numpy as jnp
import numpy as np
from jax import lax

D = 4096
FF = 14336
EXPERTS = 8
TOPK = 2
TOK_DEV = 8
CAP = 4
TOKENS = 256
N_EXPERT = 4
N_HID = 4


def place_ends(values, own_key, smallest, top_value):
    longest = values.shape.index(max(values.shape))
    spots = []
    for shift in (0, 1):
        where = [jax.random.randint(jax.random.fold_in(own_key, axis), (), 0, length) for axis, length in enumerate(values.shape)]
        where[longest] = (where[longest] + shift) % values.shape[longest]
        spots.append(tuple(where))
    return values.at[spots[0]].set(smallest).at[spots[1]].set(top_value)


def level_of(key, extent, cuts, low, high):
    loudness = 1.0
    for position, shards_of in cuts:
        draws = jax.random.uniform(jax.random.fold_in(jax.random.fold_in(key, 6), position), (shards_of,), jnp.float32, low / len(cuts), high / len(cuts))
        loudness = loudness * jnp.repeat(jnp.exp(draws), extent[position] // shards_of).reshape((-1,) + (1,) * (len(extent) - 1 - position))
    return loudness


def shared_out(key, own, number, rows, number_of, top, limit, lean):
    order = jax.random.permutation(key, number_of)
    heavy_load, common = shares(number_of, rows * top, limit, lean, True), shares(number_of, rows * top, limit, lean, False)
    places = jnp.arange(number_of)

    def named(lengths, turn):
        used = int((lengths > 0).sum())
        fixed = max(1, used // 4)
        passed = fixed + (places - fixed + turn * (used - fixed)) % max(1, number_of - fixed)
        return jnp.zeros((number_of,), jnp.int32).at[order[jnp.where(places < fixed, places, passed)]].set(jnp.asarray(lengths, jnp.int32))

    lengths = jnp.where(number % 4 == 0, named(heavy_load, number // 4), named(common, number - number // 4 - 1))
    mixed = jax.random.permutation(jax.random.fold_in(own, 3), number_of)
    donor, taker = mixed[0:number_of // 2 * 2:2], mixed[1:number_of // 2 * 2:2]
    slack = jnp.minimum(lengths[donor] - 1, limit - lengths[taker]) // 2
    slack = jnp.where((donor == order[0]) | (taker == order[0]) | (lengths[taker] == 0), 0, jnp.maximum(slack, 0))
    passed = jax.random.randint(jax.random.fold_in(own, 4), (number_of // 2,), 0, 1 << 20) % (slack + 1)
    lengths = lengths.at[donor].add(-passed).at[taker].add(passed)
    labels = jnp.searchsorted(jnp.cumsum(lengths), jnp.arange(rows * top), side="right").astype(jnp.int32)
    table = labels.reshape(top, rows).T
    table = table[jax.random.permutation(jax.random.fold_in(own, 1), rows)]
    turn = jax.random.randint(jax.random.fold_in(own, 2), (rows, 1), 0, top)
    return jnp.take_along_axis(table, (jnp.arange(top)[None, :] + turn) % top, axis=1)


def shares(count, total, bound, slope, full):
    portions = [(1 << 20) // math.isqrt(standing ** slope) + 1 for standing in range(1, count + 1)]
    largest = bound if full else min(bound, max(-(-total // count), total * portions[0] // sum(portions)))
    least = 1 if total - largest >= count - 1 else 0
    given, rest = [largest] + [least] * (count - 1), total - largest - least * (count - 1)
    while rest > 0:
        movable = [i for i in range(1, count) if given[i] < largest] or [i for i in range(1, count) if given[i] < bound]
        whole, budget = sum([portions[i] for i in movable]), rest
        for i in movable:
            extra = min(bound - given[i], max(1, budget * portions[i] // whole), rest)
            given[i] = given[i] + extra
            rest = rest - extra
    return np.array(given)


def normal_values(rng, shape, scale, limit, shards=(), held_as=jnp.bfloat16):
    array = scale * jax.random.normal(rng, shape, jnp.float32)
    if shards:
        array = array * level_of(rng, shape, shards, -0.22, 0.18)
    return jnp.clip(array, -limit, limit).astype(held_as)


def setup_inputs(seed: int = 0) -> dict:
    arg_keys = jax.random.split(jax.random.key(seed), 7)
    tokens = normal_values(arg_keys[0], (TOKENS, D), 1.0, 6.0, ((0, 32),))
    expert_ids_keys = jax.random.split(jax.random.fold_in(arg_keys[1], 1), TOKENS // TOK_DEV)
    expert_ids_turns = jax.random.permutation(jax.random.fold_in(arg_keys[1], 3), TOKENS // TOK_DEV)
    expert_ids = jax.vmap(lambda own, number: shared_out(jax.random.fold_in(arg_keys[1], 2), own, number, TOK_DEV, EXPERTS, TOPK, CAP, 2))(expert_ids_keys, expert_ids_turns).reshape((TOKENS, TOPK))
    gate_numer = place_ends(jax.random.randint(arg_keys[2], (TOKENS, TOPK), 8, 65), jax.random.fold_in(arg_keys[2], 1), 8, 64).astype(jnp.int32)
    gate_weight = normal_values(arg_keys[3], (EXPERTS, D, FF), D ** -0.5, 0.09375, ((0, 2), (2, 16)))
    up_weight = normal_values(arg_keys[4], (EXPERTS, D, FF), D ** -0.5, 0.09375, ((0, 2), (2, 16)))
    down_weight = normal_values(arg_keys[5], (EXPERTS, FF, D), FF ** -0.5, 0.046875, ((0, 2), (1, 16)))
    return dict(tokens=tokens, expert_ids=expert_ids, gate_numer=gate_numer, gate_weight=gate_weight, up_weight=up_weight, down_weight=down_weight)


def reference(tokens, expert_ids, gate_numer, gate_weight, up_weight, down_weight):
    rows = CAP * (TOKENS // TOK_DEV)
    pieces = N_EXPERT * N_HID
    width_piece = FF // pieces
    route_w = gate_numer.astype(jnp.float32) * (1.0 / 64.0)

    def one_expert(packed):
        index, w_gate, w_up, w_down = packed
        chosen = expert_ids == index
        picked = jnp.any(chosen, axis=1)
        scale = jnp.sum(jnp.where(chosen, route_w, jnp.float32(0.0)), axis=1)
        order = jnp.nonzero(picked, size=rows, fill_value=0)[0].astype(jnp.int32)
        live = (jnp.arange(rows, dtype=jnp.int32) < jnp.sum(picked.astype(jnp.int32))).astype(jnp.float32)
        rows_in = tokens[order]
        gate = jnp.dot(rows_in, w_gate, preferred_element_type=jnp.float32)
        upper = jnp.dot(rows_in, w_up, preferred_element_type=jnp.float32)
        hidden = (jax.nn.silu(gate) * upper).astype(jnp.bfloat16)
        hidden_parts = jnp.transpose(hidden.reshape(rows, pieces, width_piece), (1, 0, 2))
        down_parts = w_down.reshape(pieces, width_piece, D)

        def one_piece(carry, pair):
            left, right = pair
            partial_value = jnp.dot(left, right, preferred_element_type=jnp.float32).astype(jnp.bfloat16)
            partial_value = lax.optimization_barrier(partial_value).astype(jnp.float32)
            return carry + partial_value, None

        total, unused = lax.scan(one_piece, jnp.zeros((rows, D), jnp.float32), (hidden_parts, down_parts))
        result = total.astype(jnp.bfloat16)
        result = lax.optimization_barrier(result).astype(jnp.float32)
        factor = scale[order] * live
        return jnp.zeros((TOKENS, D), jnp.float32).at[order].add(result * factor[:, None])

    indices = jnp.arange(EXPERTS, dtype=jnp.int32)
    parts = lax.map(one_expert, (indices, gate_weight, up_weight, down_weight))
    return jnp.sum(parts, axis=0).astype(jnp.bfloat16)
```

```python
import functools

import jax
import jax.numpy as jnp
from jax import lax
from jax.experimental import pallas as pl
from jax.experimental.pallas import tpu as pltpu
from jax.sharding import PartitionSpec as P

AXES = ("group", "expert", "hid")
LANES = 128
ROW_BLOCK = 256
VMEM = 60 * 1024 * 1024


def tile_of(extent, most):
    return max(t for t in range(LANES, most + 1, LANES) if extent % t == 0)


def ffn_kernel(kt, nt, x_ref, wg, wu, wd, out_ref, gbuf, ubuf, dbuf, acc, hid, gsem, usem, dsem):
    local, width, ff = wg.shape
    nk, nn = width // kt, width // nt
    gslots, dslots = gbuf.shape[0], dbuf.shape[0]
    first = lax.axis_index("group") * local

    def gate_copies(i):
        e, k = i // nk, lax.rem(i, nk)
        s = lax.rem(i, gslots)
        rows = pl.ds(pl.multiple_of(k * kt, kt), kt)
        return (
            pltpu.make_async_copy(wg.at[e, rows, :], gbuf.at[s], gsem.at[s]),
            pltpu.make_async_copy(wu.at[e, rows, :], ubuf.at[s], usem.at[s]),
        )

    def down_copy(i):
        e, n = i // nn, lax.rem(i, nn)
        s = lax.rem(i, dslots)
        cols = pl.ds(pl.multiple_of(n * nt, nt), nt)
        return pltpu.make_async_copy(wd.at[e, :, cols], dbuf.at[s], dsem.at[s])

    def start_gate(i):
        @pl.when(i < local * nk)
        def _():
            for copy in gate_copies(i):
                copy.start()

    def start_down(i):
        @pl.when(i < local * nn)
        def _():
            down_copy(i).start()

    for i in range(min(gslots, local * nk)):
        for copy in gate_copies(jnp.int32(i)):
            copy.start()
    for i in range(min(dslots, local * nn)):
        down_copy(jnp.int32(i)).start()

    route = x_ref[:, width:].astype(jnp.float32)
    lane = lax.broadcasted_iota(jnp.int32, route.shape, 1)

    def expert(e, carry):
        def up(k, carry):
            i = e * nk + k
            s = lax.rem(i, gslots)
            for copy in gate_copies(i):
                copy.wait()
            x = x_ref[:, pl.ds(pl.multiple_of(k * kt, kt), kt)]
            gate = jnp.dot(x, gbuf[s], preferred_element_type=jnp.float32)
            upper = jnp.dot(x, ubuf[s], preferred_element_type=jnp.float32)

            @pl.when(k == 0)
            def _():
                acc[0] = gate
                acc[1] = upper

            @pl.when(k > 0)
            def _():
                acc[0] += gate
                acc[1] += upper

            start_gate(i + gslots)
            return carry

        lax.fori_loop(0, nk, up, 0)
        scale = jnp.sum(jnp.where(lane == first + e, route, 0.0), axis=1, keepdims=True)
        gate = acc[0]
        hid[...] = (gate / (1.0 + jnp.exp(-gate)) * acc[1] * scale).astype(jnp.bfloat16)

        def down(n, carry):
            i = e * nn + n
            s = lax.rem(i, dslots)
            down_copy(i).wait()
            part = jnp.dot(hid[...], dbuf[s], preferred_element_type=jnp.float32)
            cols = pl.ds(pl.multiple_of(n * nt, nt), nt)

            @pl.when(e == 0)
            def _():
                out_ref[:, cols] = part

            @pl.when(e > 0)
            def _():
                out_ref[:, cols] += part

            start_down(i + dslots)
            return carry

        lax.fori_loop(0, nn, down, 0)
        return carry

    lax.fori_loop(0, local, expert, 0)


def ffn(x, wg, wu, wd):
    rows = x.shape[0]
    local, width, ff = wg.shape
    kt, nt = tile_of(width, 512), tile_of(width, 1024)
    gslots, dslots = min(12, local * (width // kt)), min(6, local * (width // nt))
    anywhere = pl.BlockSpec(memory_space=pl.ANY)
    vmem = pl.BlockSpec(memory_space=pltpu.VMEM)
    return pl.pallas_call(
        functools.partial(ffn_kernel, kt, nt),
        out_shape=jax.ShapeDtypeStruct((rows, width), jnp.float32),
        in_specs=[vmem, anywhere, anywhere, anywhere],
        out_specs=vmem,
        scratch_shapes=[
            pltpu.VMEM((gslots, kt, ff), jnp.bfloat16),
            pltpu.VMEM((gslots, kt, ff), jnp.bfloat16),
            pltpu.VMEM((dslots, ff, nt), jnp.bfloat16),
            pltpu.VMEM((2, rows, ff), jnp.float32),
            pltpu.VMEM((rows, ff), jnp.bfloat16),
            pltpu.SemaphoreType.DMA((gslots,)),
            pltpu.SemaphoreType.DMA((gslots,)),
            pltpu.SemaphoreType.DMA((dslots,)),
        ],
        compiler_params=pltpu.CompilerParams(vmem_limit_bytes=VMEM),
        cost_estimate=pl.CostEstimate(
            flops=6 * rows * local * width * ff,
            bytes_accessed=6 * local * width * ff,
            transcendentals=rows * local * ff,
        ),
    )(x, wg, wu, wd)


def pack(tokens, expert_ids, gate_numer, experts):
    lane = jnp.arange(-(-experts // LANES) * LANES, dtype=jnp.int32)
    route = gate_numer.astype(jnp.float32) * (1.0 / 64.0)
    dense = jnp.sum(jnp.where(expert_ids[:, :, None] == lane, route[:, :, None], 0.0), axis=1)
    return jnp.concatenate([tokens, dense.astype(jnp.bfloat16)], axis=1)


def body(tokens, expert_ids, gate_numer, gate_weight, up_weight, down_weight):
    local = gate_weight.shape[0]
    experts = lax.axis_size("group") * local
    packed = pack(tokens, expert_ids, gate_numer, experts)
    x = lax.all_gather(packed, AXES, axis=0, tiled=True)
    rows = x.shape[0]
    if rows > ROW_BLOCK:
        parts = [
            ffn(x[r : r + ROW_BLOCK], gate_weight, up_weight, down_weight).astype(jnp.bfloat16)
            for r in range(0, rows, ROW_BLOCK)
        ]
        total = jnp.concatenate(parts, axis=0)
    else:
        total = ffn(x, gate_weight, up_weight, down_weight).astype(jnp.bfloat16)
    return lax.psum_scatter(total, AXES, scatter_dimension=0, tiled=True)


def solution(mesh):
    return jax.shard_map(
        body,
        mesh=mesh,
        in_specs=(
            P(AXES, None),
            P(AXES, None),
            P(AXES, None),
            P("group", None, ("expert", "hid")),
            P("group", None, ("expert", "hid")),
            P("group", ("expert", "hid"), None),
        ),
        out_specs=P(AXES, None),
        check_vma=False,
    )
```

```python
import functools

import jax
import jax.numpy as jnp
from jax import lax
from jax.experimental import pallas as pl
from jax.experimental.pallas import tpu as pltpu
from jax.sharding import PartitionSpec as P

AXES = ("group", "expert", "hid")
MEMBERS = ("expert", "hid")
LANES = 128
ROW_BLOCK = 256
VMEM = 60 * 1024 * 1024


def tile_of(extent, most):
    return max(t for t in range(LANES, most + 1, LANES) if extent % t == 0)


def ffn_kernel(kt, nt, x_ref, wg, wu, wd, out_ref, gbuf, ubuf, dbuf, acc, total, hid, gsem, usem, dsem):
    local, width, ff = wg.shape
    nk, nn = width // kt, width // nt
    gslots, dslots = gbuf.shape[0], dbuf.shape[0]
    first = lax.axis_index("group") * local

    def gate_copies(i):
        e, k = i // nk, lax.rem(i, nk)
        s = lax.rem(i, gslots)
        rows = pl.ds(pl.multiple_of(k * kt, kt), kt)
        return (
            pltpu.make_async_copy(wg.at[e, rows, :], gbuf.at[s], gsem.at[s]),
            pltpu.make_async_copy(wu.at[e, rows, :], ubuf.at[s], usem.at[s]),
        )

    def down_copy(i):
        e, n = i // nn, lax.rem(i, nn)
        s = lax.rem(i, dslots)
        cols = pl.ds(pl.multiple_of(n * nt, nt), nt)
        return pltpu.make_async_copy(wd.at[e, :, cols], dbuf.at[s], dsem.at[s])

    def start_gate(i):
        @pl.when(i < local * nk)
        def _():
            for copy in gate_copies(i):
                copy.start()

    def start_down(i):
        @pl.when(i < local * nn)
        def _():
            down_copy(i).start()

    for i in range(min(gslots, local * nk)):
        for copy in gate_copies(jnp.int32(i)):
            copy.start()
    for i in range(min(dslots, local * nn)):
        down_copy(jnp.int32(i)).start()

    route = x_ref[:, width:].astype(jnp.float32)
    lane = lax.broadcasted_iota(jnp.int32, route.shape, 1)

    def expert(e, carry):
        def up(k, carry):
            i = e * nk + k
            s = lax.rem(i, gslots)
            for copy in gate_copies(i):
                copy.wait()
            x = x_ref[:, pl.ds(pl.multiple_of(k * kt, kt), kt)]
            gate = jnp.dot(x, gbuf[s], preferred_element_type=jnp.float32)
            upper = jnp.dot(x, ubuf[s], preferred_element_type=jnp.float32)

            @pl.when(k == 0)
            def _():
                acc[0] = gate
                acc[1] = upper

            @pl.when(k > 0)
            def _():
                acc[0] += gate
                acc[1] += upper

            start_gate(i + gslots)
            return carry

        lax.fori_loop(0, nk, up, 0)
        scale = jnp.sum(jnp.where(lane == first + e, route, 0.0), axis=1, keepdims=True)
        gate = acc[0]
        hid[...] = (gate / (1.0 + jnp.exp(-gate)) * acc[1] * scale).astype(jnp.bfloat16)

        def down(n, carry):
            i = e * nn + n
            s = lax.rem(i, dslots)
            down_copy(i).wait()
            part = jnp.dot(hid[...], dbuf[s], preferred_element_type=jnp.float32)
            cols = pl.ds(pl.multiple_of(n * nt, nt), nt)

            @pl.when(e == 0)
            def _():
                total[:, cols] = part

            @pl.when((e > 0) & (e < local - 1))
            def _():
                total[:, cols] += part

            @pl.when((e > 0) & (e == local - 1))
            def _():
                out_ref[:, cols] = (total[:, cols] + part).astype(out_ref.dtype)

            if local == 1:
                out_ref[:, cols] = part.astype(out_ref.dtype)

            start_down(i + dslots)
            return carry

        lax.fori_loop(0, nn, down, 0)
        return carry

    lax.fori_loop(0, local, expert, 0)


def ffn(x, wg, wu, wd):
    rows = x.shape[0]
    local, width, ff = wg.shape
    kt, nt = tile_of(width, 1024), tile_of(width, 1024)
    gslots, dslots = min(6, local * (width // kt)), min(6, local * (width // nt))
    anywhere = pl.BlockSpec(memory_space=pl.ANY)
    vmem = pl.BlockSpec(memory_space=pltpu.VMEM)
    return pl.pallas_call(
        functools.partial(ffn_kernel, kt, nt),
        out_shape=jax.ShapeDtypeStruct((rows, width), jnp.bfloat16),
        in_specs=[vmem, anywhere, anywhere, anywhere],
        out_specs=vmem,
        scratch_shapes=[
            pltpu.VMEM((gslots, kt, ff), jnp.bfloat16),
            pltpu.VMEM((gslots, kt, ff), jnp.bfloat16),
            pltpu.VMEM((dslots, ff, nt), jnp.bfloat16),
            pltpu.VMEM((2, rows, ff), jnp.float32),
            pltpu.VMEM((rows, width), jnp.float32),
            pltpu.VMEM((rows, ff), jnp.bfloat16),
            pltpu.SemaphoreType.DMA((gslots,)),
            pltpu.SemaphoreType.DMA((gslots,)),
            pltpu.SemaphoreType.DMA((dslots,)),
        ],
        compiler_params=pltpu.CompilerParams(vmem_limit_bytes=VMEM),
        cost_estimate=pl.CostEstimate(
            flops=6 * rows * local * width * ff,
            bytes_accessed=6 * local * width * ff,
            transcendentals=rows * local * ff,
        ),
    )(x, wg, wu, wd)


def pack(tokens, expert_ids, gate_numer, experts):
    lane = jnp.arange(-(-experts // LANES) * LANES, dtype=jnp.int32)
    route = gate_numer.astype(jnp.float32) * (1.0 / 64.0)
    dense = jnp.sum(jnp.where(expert_ids[:, :, None] == lane, route[:, :, None], 0.0), axis=1)
    return jnp.concatenate([tokens, dense.astype(jnp.bfloat16)], axis=1)


def shifted(block, groups, by):
    return lax.ppermute(block, "group", [(g, (g + by) % groups) for g in range(groups)])


def body(tokens, expert_ids, gate_numer, gate_weight, up_weight, down_weight):
    local = gate_weight.shape[0]
    experts = lax.axis_size("group") * local
    packed = pack(tokens, expert_ids, gate_numer, experts)
    groups, tok = lax.axis_size("group"), tokens.shape[0]
    turned = [packed] + [shifted(packed, groups, s) for s in range(1, groups)]
    x = lax.all_gather(jnp.concatenate(turned, axis=0), MEMBERS, axis=0, tiled=True)
    rows = x.shape[0]
    parts = [
        ffn(x[r : r + ROW_BLOCK], gate_weight, up_weight, down_weight)
        for r in range(0, rows, ROW_BLOCK)
    ]
    total = parts[0] if len(parts) == 1 else jnp.concatenate(parts, axis=0)
    summed = lax.psum_scatter(total, MEMBERS, scatter_dimension=0, tiled=True)
    mixed = summed[:tok].astype(jnp.float32)
    for s in range(1, groups):
        back = shifted(summed[s * tok : (s + 1) * tok], groups, groups - s)
        mixed = mixed + back.astype(jnp.float32)
    return mixed.astype(jnp.bfloat16)


def solution(mesh):
    return jax.shard_map(
        body,
        mesh=mesh,
        in_specs=(
            P(AXES, None),
            P(AXES, None),
            P(AXES, None),
            P("group", None, ("expert", "hid")),
            P("group", None, ("expert", "hid")),
            P("group", ("expert", "hid"), None),
        ),
        out_specs=P(AXES, None),
        check_vma=False,
    )
```

```python
import functools

import jax
import jax.numpy as jnp
from jax import lax
from jax.experimental import pallas as pl
from jax.experimental.pallas import tpu as pltpu
from jax.sharding import PartitionSpec as P

AXES = ("group", "expert", "hid")
LANES = 128
ROW_BLOCK = 256
VMEM = 60 * 1024 * 1024


def tile_of(extent, most):
    return max(t for t in range(LANES, most + 1, LANES) if extent % t == 0)


def ffn_kernel(kt, nt, x_ref, wg, wu, wd, out_ref, gbuf, ubuf, dbuf, acc, total, hid, gsem, usem, dsem):
    local, width, ff = wg.shape
    nk, nn = width // kt, width // nt
    gslots, dslots = gbuf.shape[0], dbuf.shape[0]
    first = lax.axis_index("group") * local

    def gate_copies(i):
        e, k = i // nk, lax.rem(i, nk)
        s = lax.rem(i, gslots)
        rows = pl.ds(pl.multiple_of(k * kt, kt), kt)
        return (
            pltpu.make_async_copy(wg.at[e, rows, :], gbuf.at[s], gsem.at[s]),
            pltpu.make_async_copy(wu.at[e, rows, :], ubuf.at[s], usem.at[s]),
        )

    def down_copy(i):
        e, n = i // nn, lax.rem(i, nn)
        s = lax.rem(i, dslots)
        cols = pl.ds(pl.multiple_of(n * nt, nt), nt)
        return pltpu.make_async_copy(wd.at[e, :, cols], dbuf.at[s], dsem.at[s])

    def start_gate(i):
        @pl.when(i < local * nk)
        def _():
            for copy in gate_copies(i):
                copy.start()

    def start_down(i):
        @pl.when(i < local * nn)
        def _():
            down_copy(i).start()

    for i in range(min(gslots, local * nk)):
        for copy in gate_copies(jnp.int32(i)):
            copy.start()
    for i in range(min(dslots, local * nn)):
        down_copy(jnp.int32(i)).start()

    route = x_ref[:, width:].astype(jnp.float32)
    lane = lax.broadcasted_iota(jnp.int32, route.shape, 1)

    def expert(e, carry):
        def up(k, carry):
            i = e * nk + k
            s = lax.rem(i, gslots)
            for copy in gate_copies(i):
                copy.wait()
            x = x_ref[:, pl.ds(pl.multiple_of(k * kt, kt), kt)]
            gate = jnp.dot(x, gbuf[s], preferred_element_type=jnp.float32)
            upper = jnp.dot(x, ubuf[s], preferred_element_type=jnp.float32)

            @pl.when(k == 0)
            def _():
                acc[0] = gate
                acc[1] = upper

            @pl.when(k > 0)
            def _():
                acc[0] += gate
                acc[1] += upper

            start_gate(i + gslots)
            return carry

        lax.fori_loop(0, nk, up, 0)
        scale = jnp.sum(jnp.where(lane == first + e, route, 0.0), axis=1, keepdims=True)
        gate = acc[0]
        hid[...] = (gate / (1.0 + jnp.exp(-gate)) * acc[1] * scale).astype(jnp.bfloat16)

        def down(n, carry):
            i = e * nn + n
            s = lax.rem(i, dslots)
            down_copy(i).wait()
            part = jnp.dot(hid[...], dbuf[s], preferred_element_type=jnp.float32)
            cols = pl.ds(pl.multiple_of(n * nt, nt), nt)

            @pl.when(e == 0)
            def _():
                total[:, cols] = part

            @pl.when((e > 0) & (e < local - 1))
            def _():
                total[:, cols] += part

            @pl.when((e > 0) & (e == local - 1))
            def _():
                out_ref[:, cols] = (total[:, cols] + part).astype(out_ref.dtype)

            if local == 1:
                out_ref[:, cols] = part.astype(out_ref.dtype)

            start_down(i + dslots)
            return carry

        lax.fori_loop(0, nn, down, 0)
        return carry

    lax.fori_loop(0, local, expert, 0)


def ffn(x, wg, wu, wd):
    rows = x.shape[0]
    local, width, ff = wg.shape
    kt, nt = tile_of(width, 1024), tile_of(width, 1024)
    gslots, dslots = min(6, local * (width // kt)), min(6, local * (width // nt))
    anywhere = pl.BlockSpec(memory_space=pl.ANY)
    vmem = pl.BlockSpec(memory_space=pltpu.VMEM)
    return pl.pallas_call(
        functools.partial(ffn_kernel, kt, nt),
        out_shape=jax.ShapeDtypeStruct((rows, width), jnp.bfloat16),
        in_specs=[vmem, anywhere, anywhere, anywhere],
        out_specs=vmem,
        scratch_shapes=[
            pltpu.VMEM((gslots, kt, ff), jnp.bfloat16),
            pltpu.VMEM((gslots, kt, ff), jnp.bfloat16),
            pltpu.VMEM((dslots, ff, nt), jnp.bfloat16),
            pltpu.VMEM((2, rows, ff), jnp.float32),
            pltpu.VMEM((rows, width), jnp.float32),
            pltpu.VMEM((rows, ff), jnp.bfloat16),
            pltpu.SemaphoreType.DMA((gslots,)),
            pltpu.SemaphoreType.DMA((gslots,)),
            pltpu.SemaphoreType.DMA((dslots,)),
        ],
        compiler_params=pltpu.CompilerParams(vmem_limit_bytes=VMEM),
        cost_estimate=pl.CostEstimate(
            flops=6 * rows * local * width * ff,
            bytes_accessed=6 * local * width * ff,
            transcendentals=rows * local * ff,
        ),
    )(x, wg, wu, wd)


def pack(tokens, expert_ids, gate_numer, experts):
    lane = jnp.arange(-(-experts // LANES) * LANES, dtype=jnp.int32)
    route = gate_numer.astype(jnp.float32) * (1.0 / 64.0)
    dense = jnp.sum(jnp.where(expert_ids[:, :, None] == lane, route[:, :, None], 0.0), axis=1)
    return jnp.concatenate([tokens, dense.astype(jnp.bfloat16)], axis=1)


def swapped(block, axis, bit):
    pairs = [(i, i ^ bit) for i in range(lax.axis_size(axis))]
    return lax.ppermute(block, axis, pairs)


def bits(axis):
    size = lax.axis_size(axis)
    return [1 << b for b in reversed(range(size.bit_length() - 1))]


def body(tokens, expert_ids, gate_numer, gate_weight, up_weight, down_weight):
    local = gate_weight.shape[0]
    experts = lax.axis_size("group") * local
    packed = pack(tokens, expert_ids, gate_numer, experts)
    steps = [(axis, bit) for axis in ("expert", "group", "hid") for bit in bits(axis)]
    x = packed
    for axis, bit in steps:
        x = jnp.concatenate([x, swapped(x, axis, bit)], axis=0)
    rows = x.shape[0]
    parts = [
        ffn(x[r : r + ROW_BLOCK], gate_weight, up_weight, down_weight)
        for r in range(0, rows, ROW_BLOCK)
    ]
    total = parts[0] if len(parts) == 1 else jnp.concatenate(parts, axis=0)
    for axis, bit in reversed(steps):
        half = total.shape[0] // 2
        back = swapped(total[half:], axis, bit)
        total = (total[:half].astype(jnp.float32) + back.astype(jnp.float32)).astype(jnp.bfloat16)
    return total


def solution(mesh):
    return jax.shard_map(
        body,
        mesh=mesh,
        in_specs=(
            P(AXES, None),
            P(AXES, None),
            P(AXES, None),
            P("group", None, ("expert", "hid")),
            P("group", None, ("expert", "hid")),
            P("group", ("expert", "hid"), None),
        ),
        out_specs=P(AXES, None),
        check_vma=False,
    )
```
